32 devices in a mesh: ccd: 16 (over z, y, x), strip: 2 (over core).
Axes of the slice: x: 2, y: 2, z: 4, core: 2. Of those that a mesh axis runs over, the one named last changes fastest.
Arguments:
- coadd_blocks: bfloat16 [4096, 512], P(('ccd', 'strip')), may hold values from -10.5 to 10.5
- block_route: int32 [1024, 1], P(('ccd', 'strip')), may hold values from 0 to 31, as said below
- block_offset: int32 [1024], P(('ccd', 'strip')), may hold values from 0 to 380
- warp_matrix: bfloat16 [8192, 384], P(('ccd', 'strip')), may hold values from -0.1875 to 0.1875
- science: float32 [8192, 512], P(('ccd', 'strip')), may hold values from -6 to 6
- basis_columns: bfloat16 [21, 21], replicated, may hold values from -0.375 to 0.375
- basis_rows: bfloat16 [21, 21], replicated, may hold values from -0.375 to 0.375
- stamp_corner: int32 [256, 2], P(('ccd', 'strip')), may hold values from 0 to 480, as said below
- stamp_count: int32 [32], P(('ccd', 'strip')), may hold values from 1 to 8, as said below
- kernel_prior: float32 [132], replicated, may hold values from -4 to 4
Outputs:
- difference: float32 [8192, 512], P(('ccd', 'strip'))
- stamp_residuals: float32 [256, 1024], P(('ccd', 'strip'))
- kernel_solution: float32 [132], replicated
The draws below stay inside these ranges and needn't reach their ends.
Inputs may be any that keep to these rules, and one draw needn't show every extreme that they name: `block_route`: among the 32 blocks of one device at most 2 name the same device, and in every draw some device is named exactly 2 times by the blocks of every device. `stamp_corner`: every stamp lies inside its strip (row corners at most 224, column corners at most 480), and the stamps of one device never intersect. `stamp_count`: some device has all 8 slots live.
All inputs are finite; a program needn't handle non-finite values.
Results may differ from the reference program's by a relative error of at most 0.002.
The reference program's roundings to bfloat16 on the way (of `source_frame`, `template`, `across`, `convolved` and `features`) count: a program that leaves them out, or rounds other values in their place, can miss the bound.
Values may be sent and summed in bfloat16 or wider, within the bound.
A program may use at most 128 MiB of HBM per device.

```python
import math
import jax
import jax.numpy as jnp
from jax import lax

R = 256
C = 512
NS = 8
BR = 4
KH = 10
NK = 21
NPOLY = 6
SS = 32
CELL = 64
NB = 32
RS = 384
KS = 21
NU = 132
N_CCD = 16
N_STRIP = 2


def route_table(key):
    processor_number = N_CCD * N_STRIP
    class_key, forced_key, jitter_key, order_key = jax.random.split(jax.random.fold_in(key, 11), 4)
    demand_category = jax.random.randint(class_key, (processor_number,), 0, 8)
    forced_choice = jax.random.randint(forced_key, (), 0, processor_number)
    preference_boost = jnp.where(demand_category == 0, 131072, jnp.where(demand_category < 3, 32768, jnp.where(demand_category < 5, 16384, 0)))
    preference_boost = jnp.where(jnp.arange(processor_number, dtype=jnp.int32) == forced_choice, 262144, preference_boost).astype(jnp.int32)
    slot_holder = jnp.concatenate([jnp.arange(processor_number, dtype=jnp.int32), jnp.arange(processor_number, dtype=jnp.int32)])
    random_perturbation = jax.random.randint(jitter_key, (processor_number, 2 * processor_number), 0, 65536).astype(jnp.int32)
    ranking_scores = (random_perturbation + preference_boost[slot_holder][None, :]) * (2 * processor_number) + jnp.arange(2 * processor_number, dtype=jnp.int32)[None, :]
    _, picked = lax.top_k(ranking_scores, NB)
    chosen = slot_holder[picked]
    shuffled = jax.vmap(jax.random.permutation)(jax.random.split(order_key, processor_number), chosen)
    return shuffled.reshape(processor_number * NB).astype(jnp.int32)


def offset_table(key):
    block_total = N_CCD * N_STRIP * NB
    offsets = jax.random.randint(jax.random.fold_in(key, 12), (block_total,), 0, RS - BR + 1).astype(jnp.int32)
    return offsets.at[0].set(RS - BR).at[1].set(0)


def coadd_values(key):
    base_key, scale_key = jax.random.split(jax.random.fold_in(key, 13))
    block_total = N_CCD * N_STRIP * NB
    scales = jnp.exp(jax.random.uniform(scale_key, (block_total, 1, 1), jnp.float32, math.log(0.3), math.log(3.0)))
    values = jnp.clip(jax.random.normal(base_key, (block_total, BR, C), jnp.float32), -3.5, 3.5)
    return (values * scales).reshape(block_total * BR, C)


def warp_values(key):
    processor_number = N_CCD * N_STRIP
    values = jax.random.normal(jax.random.fold_in(key, 14), (processor_number * R, RS), jnp.float32) * RS ** (-0.5)
    return jnp.clip(values, -0.1875, 0.1875).astype(jnp.bfloat16)


def basis_values(key, constant_tag):
    values = jax.random.normal(jax.random.fold_in(key, constant_tag), (NK, KS), jnp.float32) * KS ** (-0.5)
    return jnp.clip(values, -0.375, 0.375).astype(jnp.bfloat16)


def polynomial_field(coefficient, yvalue, xvalue):
    return coefficient[0] + coefficient[1] * xvalue + coefficient[2] * yvalue + coefficient[3] * (1.5 * xvalue * xvalue - 0.5) + coefficient[4] * (xvalue * yvalue) + coefficient[5] * (1.5 * yvalue * yvalue - 0.5)


def draw_block_route(key, part):
    return route_table(key).reshape(-1, 1)


def draw_block_offset(key, part):
    return offset_table(key)


def draw_coadd_blocks(key, part):
    return coadd_values(key).astype(jnp.bfloat16)


def draw_warp_matrix(key, part):
    return warp_values(key)


def draw_basis_columns(key, part):
    return basis_values(key, 15)


def draw_basis_rows(key, part):
    return basis_values(key, 16)


def draw_science(key, part):
    processor_number = N_CCD * N_STRIP
    total_rows = processor_number * R
    landing = route_table(key) * RS + offset_table(key)
    landing_rows = (landing[:, None] + jnp.arange(BR, dtype=jnp.int32)[None, :]).reshape(-1)
    coadd_rows = coadd_values(key).astype(jnp.bfloat16).astype(jnp.float32)
    source_frame = jnp.zeros((processor_number * RS, C), jnp.float32).at[landing_rows].add(coadd_rows)
    warp_field = warp_values(key).astype(jnp.float32).reshape(processor_number, R, RS)
    template = jnp.einsum('drs,dsc->drc', warp_field, source_frame.reshape(processor_number, RS, C), precision=lax.Precision.HIGHEST).reshape(total_rows, C)
    padded = jnp.pad(template, KH)
    column_taps = basis_values(key, 15).astype(jnp.float32)
    row_taps = basis_values(key, 16).astype(jnp.float32)
    truth_key, noise_key = jax.random.split(jax.random.fold_in(key, 17))
    truth_table = 0.12 * jax.random.normal(truth_key, (NK + 1, 6), jnp.float32)
    noise_field = 0.5 * jax.random.normal(noise_key, (total_rows, C), jnp.float32)
    truth_table = truth_table.at[NK].multiply(4.0)
    ycoord = ((2 * jnp.arange(total_rows, dtype=jnp.int32) + 1).astype(jnp.float32) / total_rows - 1.0)[:, None]
    xcoord = ((2 * jnp.arange(C, dtype=jnp.int32) + 1).astype(jnp.float32) / C - 1.0)[None, :]

    def add_kernel(model_sum, element):
        across = jnp.zeros((total_rows + 2 * KH, C), jnp.float32)
        for offset in range(KS):
            across = across + element[0][offset] * padded[:, offset:offset + C]
        matched = jnp.zeros((total_rows, C), jnp.float32)
        for offset in range(KS):
            matched = matched + element[1][offset] * across[offset:offset + total_rows, :]
        return (model_sum + matched * polynomial_field(element[2], ycoord, xcoord), None)
    starting = polynomial_field(truth_table[NK], ycoord, xcoord)
    model_sum, _ = lax.scan(add_kernel, starting, (column_taps, row_taps, truth_table[:NK]))
    return jnp.clip(model_sum + noise_field, -6.0, 6.0)


def draw_stamp_corner(key, part):
    cell_key, jitter_key = jax.random.split(key)
    processor_number = N_CCD * N_STRIP
    cells_down = R // CELL
    cells_across = C // CELL
    last_cell = cells_down * cells_across - 1
    chosen = jax.vmap(lambda single: jax.random.permutation(single, cells_down * cells_across)[:NS])(jax.random.split(cell_key, processor_number))
    has_last = jnp.any(chosen[0] == last_cell)
    chosen = chosen.at[0, 0].set(jnp.where(has_last, chosen[0, 0], last_cell))
    random_perturbation = jax.random.randint(jitter_key, (processor_number, NS, 2), 0, CELL - SS + 1)
    at_last = chosen[0] == last_cell
    random_perturbation = random_perturbation.at[0, :, 0].set(jnp.where(at_last, CELL - SS, random_perturbation[0, :, 0]))
    random_perturbation = random_perturbation.at[0, :, 1].set(jnp.where(at_last, CELL - SS, random_perturbation[0, :, 1]))
    corner_row = chosen // cells_across * CELL + random_perturbation[:, :, 0]
    corner_column = chosen % cells_across * CELL + random_perturbation[:, :, 1]
    return jnp.stack([corner_row, corner_column], axis=-1).reshape(processor_number * NS, 2).astype(jnp.int32)


def draw_stamp_count(key, part):
    first_key, second_key, third_key = jax.random.split(key, 3)
    processor_number = N_CCD * N_STRIP
    counts = jax.random.randint(first_key, (processor_number,), 1, NS + 1)
    fullest = jax.random.randint(second_key, (), 0, processor_number)
    sparsest = jax.random.randint(third_key, (), 0, processor_number)
    counts = counts.at[sparsest].set(1)
    return counts.at[fullest].set(NS).astype(jnp.int32)


def scatter_about(own_key, extent, width, most, held_as=jnp.bfloat16):
    return jnp.clip(width * jax.random.normal(own_key, extent, jnp.float32), -most, most).astype(held_as)


def setup_inputs(seed: int = 0) -> dict:
    arg_keys = jax.random.split(jax.random.key(seed), 11)
    return {
        "coadd_blocks": draw_coadd_blocks(jax.random.fold_in(arg_keys[10], 71), 0),
        "block_route": draw_block_route(jax.random.fold_in(arg_keys[10], 71), 0),
        "block_offset": draw_block_offset(jax.random.fold_in(arg_keys[10], 71), 0),
        "warp_matrix": draw_warp_matrix(jax.random.fold_in(arg_keys[10], 71), 0),
        "science": draw_science(jax.random.fold_in(arg_keys[10], 71), 0),
        "basis_columns": draw_basis_columns(jax.random.fold_in(arg_keys[10], 71), 0),
        "basis_rows": draw_basis_rows(jax.random.fold_in(arg_keys[10], 71), 0),
        "stamp_corner": draw_stamp_corner(jax.random.fold_in(arg_keys[10], 71), 0),
        "stamp_count": draw_stamp_count(jax.random.fold_in(arg_keys[10], 71), 0),
        "kernel_prior": scatter_about(arg_keys[9], (NU,), 0.3, 4.0, jnp.float32),
    }


def band_convolve(image_field, weights, direction, length):
    running = jnp.zeros_like(lax.slice_in_dim(image_field, 0, length, axis=direction))
    for offset in range(weights.shape[0]):
        running = running + weights[offset] * lax.slice_in_dim(image_field, offset, offset + length, axis=direction)
    return running


def legendre_terms(yvalue, xvalue):
    filler = jnp.zeros_like(yvalue + xvalue)
    return jnp.stack([filler + 1.0, filler + xvalue, filler + yvalue, filler + 1.5 * xvalue * xvalue - 0.5, filler + xvalue * yvalue, filler + 1.5 * yvalue * yvalue - 0.5])


def polynomial_sum(coefficient, yvalue, xvalue):
    return (coefficient[0] + coefficient[1] * xvalue + coefficient[2] * yvalue + coefficient[3] * (1.5 * xvalue * xvalue - 0.5)
            + coefficient[4] * (xvalue * yvalue) + coefficient[5] * (1.5 * yvalue * yvalue - 0.5))


def feature_rows(convolved, polynomials):
    products = (convolved.astype(jnp.float32)[:, None, :] * polynomials[None, :, :]).astype(jnp.bfloat16)
    return jnp.concatenate([products.reshape(-1, polynomials.shape[1]), polynomials.astype(jnp.bfloat16)], axis=0)


def fit_terms(features, weights, targets):
    weighted = features * weights.astype(jnp.bfloat16)[None, :]
    normal_matrix = lax.dot_general(weighted, features, (((1,), (1,)), ((), ())), preferred_element_type=jnp.float32)
    right_side = jnp.dot(features.astype(jnp.float32), weights * targets, precision=lax.Precision.HIGHEST)
    return normal_matrix, right_side


def spd_solve(system, wanted):
    order = system.shape[0]
    position = jnp.arange(order, dtype=jnp.int32)

    def eliminate(step, carry):
        matrix, vector = carry
        marker = (position == step).astype(matrix.dtype)
        pivot_row = jnp.sum(matrix * marker[:, None], axis=0)
        pivot_column = jnp.sum(matrix * marker[None, :], axis=1)
        pivot = jnp.sum(pivot_row * marker)
        pivot_value = jnp.sum(vector * marker)
        factor = (pivot_column / pivot) * (1.0 - marker)
        return matrix - factor[:, None] * pivot_row[None, :], vector - factor * pivot_value

    matrix, vector = lax.fori_loop(0, order, eliminate, (system, wanted))
    diagonal = jnp.sum(matrix * jnp.eye(order, dtype=matrix.dtype), axis=1)
    return vector / diagonal


def solve_fit(normal_matrix, right_side, pixels, kernel_prior):
    system = normal_matrix / pixels + jnp.eye(normal_matrix.shape[0], dtype=jnp.float32)
    wanted = right_side / pixels + kernel_prior
    return spd_solve(system, wanted)


def reference(coadd_blocks, block_route, block_offset, warp_matrix, science, basis_columns, basis_rows, stamp_corner, stamp_count, kernel_prior):
    processor_number = N_CCD * N_STRIP
    total_rows = processor_number * R
    half_width = KH
    starts = block_route[:, 0].astype(jnp.int32) * RS + block_offset.astype(jnp.int32)
    target_rows = (starts[:, None] + jnp.arange(BR, dtype=jnp.int32)[None, :]).reshape(processor_number, NB * BR)
    pieces = coadd_blocks.reshape(processor_number, NB * BR, C)

    def add_block(frame_sum, element):
        return frame_sum.at[element[1]].add(element[0].astype(jnp.float32)), None

    source_frame, _ = lax.scan(add_block, jnp.zeros((processor_number * RS, C), jnp.float32), (pieces, target_rows))
    source_frame = source_frame.astype(jnp.bfloat16).reshape(processor_number, RS, C)

    def warp_one(element):
        return jnp.dot(element[0], element[1], preferred_element_type=jnp.float32).astype(jnp.bfloat16)

    template = lax.map(warp_one, (warp_matrix.reshape(processor_number, R, RS), source_frame)).reshape(total_rows, C)
    padded = jnp.pad(template.astype(jnp.float32), ((half_width, half_width), (half_width, half_width)))

    def convolve(kernel_pair):
        across = band_convolve(padded, kernel_pair[0].astype(jnp.float32), 1, C)
        across = lax.optimization_barrier(across.astype(jnp.bfloat16)).astype(jnp.float32)
        return band_convolve(across, kernel_pair[1].astype(jnp.float32), 0, total_rows).astype(jnp.bfloat16)

    slot_index = jnp.arange(processor_number * NS, dtype=jnp.int32)
    device_of = slot_index // NS
    live_slot = (slot_index % NS) < stamp_count.astype(jnp.int32)[device_of]
    first_row = device_of * R + stamp_corner[:, 0].astype(jnp.int32)
    stamp_rows = first_row[:, None] + jnp.arange(SS, dtype=jnp.int32)[None, :]
    stamp_columns = stamp_corner[:, 1].astype(jnp.int32)[:, None] + jnp.arange(SS, dtype=jnp.int32)[None, :]

    def stamps_of(kernel_pair):
        convolved = convolve(kernel_pair)
        return convolved[stamp_rows[:, :, None], stamp_columns[:, None, :]]

    stamp_conv = lax.map(stamps_of, (basis_columns, basis_rows))
    yvalue = ((2 * stamp_rows + 1).astype(jnp.float32) / total_rows - 1.0)[:, :, None]
    xvalue = ((2 * stamp_columns + 1).astype(jnp.float32) / C - 1.0)[:, None, :]
    polynomials = legendre_terms(yvalue, xvalue)
    stamp_pixels = NS * SS * SS
    weights = jnp.broadcast_to(live_slot.astype(jnp.float32)[:, None, None], (processor_number * NS, SS, SS))
    targets = science[stamp_rows[:, :, None], stamp_columns[:, None, :]]
    conv_device = stamp_conv.reshape(NK, processor_number, stamp_pixels).transpose(1, 0, 2)
    poly_device = polynomials.reshape(NPOLY, processor_number, stamp_pixels).transpose(1, 0, 2)

    def device_fit(partial_value, element):
        normal_part, right_part = fit_terms(feature_rows(element[0], element[1]), element[2], element[3])
        return (partial_value[0] + normal_part, partial_value[1] + right_part), None

    zero_sums = (jnp.zeros((NU, NU), jnp.float32), jnp.zeros((NU,), jnp.float32))
    (normal_matrix, right_side), _ = lax.scan(device_fit, zero_sums, (conv_device, poly_device, weights.reshape(processor_number, stamp_pixels), targets.reshape(processor_number, stamp_pixels)))
    pixels = jnp.sum(stamp_count).astype(jnp.float32) * (SS * SS)
    solution = solve_fit(normal_matrix, right_side, pixels, kernel_prior)

    row_coord = ((2 * jnp.arange(total_rows, dtype=jnp.int32) + 1).astype(jnp.float32) / total_rows - 1.0)[:, None]
    column_coord = ((2 * jnp.arange(C, dtype=jnp.int32) + 1).astype(jnp.float32) / C - 1.0)[None, :]
    coefficient = solution[: NK * NPOLY].reshape(NK, NPOLY)

    def add_kernel(matched, element):
        convolved = convolve((element[0], element[1]))
        return matched + convolved.astype(jnp.float32) * polynomial_sum(element[2], row_coord, column_coord), None

    background = polynomial_sum(solution[NK * NPOLY:], row_coord, column_coord)
    matched, _ = lax.scan(add_kernel, background, (basis_columns, basis_rows, coefficient))
    difference = science - matched
    residuals = difference[stamp_rows[:, :, None], stamp_columns[:, None, :]] * live_slot.astype(jnp.float32)[:, None, None]
    return (difference, residuals.reshape(processor_number * NS, SS * SS), solution)
```

```python
import functools

import jax
import jax.numpy as jnp
from jax import lax
from jax.experimental import pallas as pl
from jax.experimental.pallas import tpu as pltpu
from jax.sharding import PartitionSpec as P

SS = 32
NK = 21
KP = 24
NF = 6 * KP
NG = NF + 16
LP = 64
RP = 16
NT = (((1,), (1,)), ((), ()))
F32 = jnp.float32
BF16 = jnp.bfloat16


def iota(shape, dim):
    return lax.broadcasted_iota(jnp.int32, shape, dim)


def toeplitz(taps_ref, k):
    row = taps_ref[pl.ds(k, 1), :]
    return pltpu.roll(jnp.broadcast_to(row, (16, 256)), 0, 1, stride=1, stride_axis=0)


def build_stamp_bands(cols_ref, rows_ref, sc_ref, sr_ref):
    def one(k, carry):
        col, row = toeplitz(cols_ref, k), toeplitz(rows_ref, k)
        for s in range(4):
            for g in range(2):
                shift = 64 * s + 16 * g
                value = col if shift == 0 else pltpu.roll(col, shift, 1)
                sc_ref[k, 32 * s + 16 * g : 32 * s + 16 * g + 16, :] = value.astype(BF16)
        for h in range(2):
            for g in range(2):
                value = pltpu.roll(row, 64 * h + 16 * g + 6, 1)[:, :128]
                sr_ref[k, 32 * h + 16 * g : 32 * h + 16 * g + 16, :] = value.astype(BF16)
        return carry

    lax.fori_loop(0, NK, one, 0)


def build_full_bands(cols_ref, rows_ref, fc_ref, fr_ref):
    def one(k, carry):
        col, row = toeplitz(cols_ref, k), toeplitz(rows_ref, k)
        for g in range(8):
            fc_ref[k, 16 * g : 16 * g + 16, :] = pltpu.roll(col, LP - 10 + 16 * g, 1).astype(BF16)
            fr_ref[k, 16 * g : 16 * g + 16, :] = pltpu.roll(row, 6 + 16 * g, 1).astype(BF16)
        return carry

    lax.fori_loop(0, NK, one, 0)


def prepare_stamps(
    first_row, total_rows, corner_ref, count_ref, science_ref,
    pick_rows_ref, pick_columns_ref, field_ref, poly_ref, target_ref,
):
    height, width = science_ref.shape
    full = pick_columns_ref.shape[1]
    live = jnp.zeros((64, 128), F32)
    rows = jnp.zeros((64, 128), jnp.int32)
    columns = jnp.zeros((64, 128), jnp.int32)
    group = iota((1, 128), 1) // 32
    half_of = iota((64, 128), 0) // 32
    lag = iota((64, height + 2 * RP), 1) - iota((64, height + 2 * RP), 0)
    short = iota((32, height), 1) - iota((32, height), 0)
    left = iota((full, 128), 0) - iota((full, 128), 1) % 64 - (LP - 10)
    side = iota((full, 128), 1) // 64
    near = iota((width, 128), 0) - iota((width, 128), 1) % 32
    value = science_ref[...]
    parts = []
    for part in range(3):
        parts.append(value.astype(BF16))
        value = value - parts[-1].astype(F32)
    picks = []
    for slot in range(8):
        a = corner_ref[slot, 0]
        e = corner_ref[slot, 1]
        picks.append((short == a).astype(F32))
        pick_rows_ref[64 * slot : 64 * slot + 64, :] = (lag == a).astype(F32).astype(BF16)
        pick_columns_ref[slot] = ((left == e) & (side == slot % 2)).astype(F32).astype(BF16)
        here = (half_of == slot // 4) & (group == slot % 4)
        live = jnp.where(here, (slot < count_ref[0]).astype(F32), live)
        rows = jnp.where(here, a, rows)
        columns = jnp.where(here, e, columns)
    picks = jnp.concatenate(picks, axis=0).astype(BF16)
    picked = jnp.dot(picks, jnp.concatenate(parts, axis=1), preferred_element_type=F32).astype(BF16)
    for h in range(2):
        total = jnp.zeros((96, 128), F32)
        for s in range(4):
            slot = h * 4 + s
            stack = jnp.concatenate(
                [
                    picked[32 * slot : 32 * slot + 32, width * part : width * part + width]
                    for part in range(3)
                ],
                axis=0,
            )
            chosen = ((near == corner_ref[slot, 1]) & (group == s)).astype(F32).astype(BF16)
            total = total + jnp.dot(stack, chosen, preferred_element_type=F32)
        for part in range(3):
            at = slice(32 * h, 32 * h + 32)
            target_ref[part, at, :] = total[32 * part : 32 * part + 32] * live[at]
    for part in range(3, 16):
        target_ref[part] = jnp.zeros((64, 128), F32)
    rows = rows + iota((64, 128), 0) % 32 + first_row
    columns = columns + iota((64, 128), 1) % 32
    y = (2 * rows + 1).astype(F32) / total_rows - 1.0
    x = (2 * columns + 1).astype(F32) / width - 1.0
    poly_ref[0] = jnp.ones_like(x)
    poly_ref[1] = x
    poly_ref[2] = y
    poly_ref[3] = 1.5 * x * x - 0.5
    poly_ref[4] = x * y
    poly_ref[5] = 1.5 * y * y - 0.5
    field_ref[NK] = live
    for k in range(NK + 1, KP):
        field_ref[k] = jnp.zeros((64, 128), F32)


def stamp_gram(
    ext_ref, pick_rows_ref, pick_columns_ref, sc_ref, sr_ref,
    x2_ref, field_ref, poly_ref, target_ref, gram_ref,
):
    picked = jnp.dot(pick_rows_ref[...], ext_ref[...], preferred_element_type=F32).astype(BF16)
    for pair in range(4):
        window = sum(
            jnp.dot(
                picked[64 * slot : 64 * slot + 64], pick_columns_ref[slot],
                preferred_element_type=F32,
            )
            for slot in (2 * pair, 2 * pair + 1)
        )
        at = 128 * (pair % 2)
        x2_ref[64 * (pair // 2) : 64 * (pair // 2) + 64, at : at + 128] = window.astype(BF16)
    live = field_ref[NK]

    def convolve(k, carry):
        across = lax.dot_general(x2_ref[...], sc_ref[k], NT, preferred_element_type=F32)
        down = jnp.dot(sr_ref[k], across.astype(BF16), preferred_element_type=F32)
        field_ref[k] = down.astype(BF16).astype(F32) * live
        return carry

    lax.fori_loop(0, NK, convolve, 0)
    gram_ref[...] = jnp.zeros_like(gram_ref)

    def row_features(q):
        field = field_ref[:, q, :]
        parts = [field]
        for p in range(1, 6):
            parts.append(field * poly_ref[p, pl.ds(q, 1), :])
        parts.append(target_ref[:, q, :])
        return jnp.concatenate(parts, axis=0).astype(BF16)

    def add(step, carry):
        both = jnp.concatenate([row_features(2 * step), row_features(2 * step + 1)], axis=1)
        gram_ref[:, :NG] += lax.dot_general(both, both, NT, preferred_element_type=F32)
        return carry

    lax.fori_loop(0, 32, add, 0)


def full_convolution(ext_ref, fc_ref, fr_ref, across_ref, conv_ref, first, last):
    tiles = conv_ref.shape[2] // 128
    halves = conv_ref.shape[1] // 128

    def one(k, carry):
        for t in range(tiles):
            across_ref[:, 128 * t : 128 * t + 128] = lax.dot_general(
                ext_ref[:, 128 * t : 128 * t + 256], fc_ref[k], NT, preferred_element_type=F32
            ).astype(BF16)
        for t in range(halves):
            conv_ref[k, 128 * t : 128 * t + 128, :] = jnp.dot(
                fr_ref[k, :, :160],
                across_ref[128 * t : 128 * t + 160, :],
                preferred_element_type=F32,
            ).astype(BF16)
        return carry

    lax.fori_loop(first, last, one, 0)


def solve(sum_ref, prior_ref, system_ref, answer_ref, solution_ref):
    at = iota((NF, 256), 0)
    lane = iota((NF, 256), 1)
    left = sum_ref[: NG // 8].reshape(NG, 128)
    corner = sum_ref[NG // 8 :].reshape(NG - 128, 128)
    edge = jnp.concatenate([left[128:], jnp.zeros((256 - NG, 128), F32)], axis=0)
    right = jnp.concatenate([edge.T, corner[: NF - 128]], axis=0)
    wide = jnp.concatenate([left[:NF], right], axis=1)
    pixels = left[NK : NK + 1, NK : NK + 1]
    order = (at % KP) * 6 + at // KP
    used = at % KP <= NK
    right = jnp.sum(jnp.where((lane >= NF) & (lane < NF + 3), wide, 0.0), axis=1, keepdims=True)
    prior = jnp.sum(
        jnp.where((lane == order) & used, prior_ref[...], 0.0), axis=1, keepdims=True
    )
    right = right / pixels + prior
    body = jnp.where(used & (lane % KP <= NK) & (lane < NF), wide / pixels, 0.0)
    body = body + (at == lane).astype(F32)
    system_ref[...] = jnp.where((lane == NF) & used, right, body)

    def eliminate(j, carry):
        matrix = system_ref[...]
        row = system_ref[pl.ds(j, 1), :]
        column = jnp.sum(jnp.where(lane == j, matrix, 0.0), axis=1, keepdims=True)
        pivot = jnp.sum(jnp.where(lane[:1] == j, row, 0.0), axis=1, keepdims=True)
        factor = jnp.where(at[:, :1] == j, 0.0, column / pivot)
        system_ref[...] = matrix - factor * row
        return carry

    lax.fori_loop(0, NF, eliminate, 0)
    matrix = system_ref[...]
    top = jnp.sum(jnp.where(lane == NF, matrix, 0.0), axis=1, keepdims=True)
    diagonal = jnp.sum(jnp.where(lane == at, matrix, 0.0), axis=1, keepdims=True)
    answer = top / diagonal
    answer_ref[...] = jnp.broadcast_to(answer, (NF, 128))
    solution_ref[...] = jnp.sum(
        jnp.where((lane == order) & used, answer, 0.0), axis=0, keepdims=True
    )


def subtract(
    first_row, total_rows, science_ref, conv_ref, answer_ref, difference_ref,
):
    height, width = science_ref.shape
    x = (2 * iota((1, width), 1) + 1).astype(F32) / width - 1.0
    x2 = 1.5 * x * x - 0.5

    def band(step, carry):
        start = pl.multiple_of(step * 16, 16)
        y = (2 * (first_row + start + iota((16, 128), 0)) + 1).astype(F32) / total_rows - 1.0
        y2 = 1.5 * y * y - 0.5

        def term(k):
            c = [answer_ref[p * KP + k : p * KP + k + 1, :] for p in range(6)]
            flat, slope, curve = c[0] + c[2] * y + c[5] * y2, c[1] + c[4] * y, c[3]
            spread = lambda v: jnp.concatenate([v] * (width // 128), axis=1)
            return spread(flat), spread(slope), spread(curve)

        flat, slope, curve = term(NK)
        curve = jnp.broadcast_to(curve, flat.shape)
        for k in range(NK):
            value = conv_ref[k, pl.ds(start, 16), :].astype(F32)
            f, s, c = term(k)
            flat, slope, curve = flat + value * f, slope + value * s, curve + value * c
        matched = flat + slope * x + curve * x2
        difference_ref[pl.ds(start, 16), :] = science_ref[pl.ds(start, 16), :] - matched
        return carry

    lax.fori_loop(0, height // 16, band, 0)


def stamp_residuals(answer_ref, field_ref, poly_ref, target_ref, piece_ref, residual_ref):
    value = target_ref[0] + target_ref[1] + target_ref[2]
    for k in range(NK + 1):
        weight = answer_ref[k : k + 1, :]
        for p in range(1, 6):
            weight = weight + answer_ref[p * KP + k : p * KP + k + 1, :] * poly_ref[p]
        value = value - field_ref[k] * weight
    group = iota((8, 128), 1) // 32
    for slot in range(8):
        s = slot % 4
        piece = value[32 * (slot // 4) : 32 * (slot // 4) + 32]
        piece_ref[...] = pltpu.roll(piece, 128 - 32 * s, 1) if s else piece
        result = jnp.zeros((8, 128), F32)
        for m in range(4):
            part = piece_ref[pl.ds(m, 8, stride=4), :]
            part = pltpu.roll(part, 32 * m, 1) if m else part
            result = jnp.where(group == m, part, result)
        residual_ref[slot] = result


MESH = pl.DeviceIdType.MESH
TILES = NG // 8 + (NG - 128) // 8


def coords(device):
    return (device // lax.axis_size("strip"), lax.rem(device, lax.axis_size("strip")))


def send(src, dst, send_sem, recv_sem, device):
    pltpu.make_async_remote_copy(
        src_ref=src, dst_ref=dst, send_sem=send_sem, recv_sem=recv_sem,
        device_id=coords(device), device_id_type=MESH,
    ).start()


def await_bytes(ref, sem):
    pltpu.make_async_copy(ref, ref, sem).wait()


def pack(total, blocks_ref, route_ref, offset_ref, out_ref, spot_ref):
    count = route_ref.shape[0]
    height = blocks_ref.shape[0] // count
    goal = route_ref[...].astype(F32)
    down, along = iota((count, count), 0), iota((count, count), 1)
    goal_row = jnp.sum(jnp.where(down == along, goal, 0.0), axis=0, keepdims=True)
    same = goal == goal_row
    rank = jnp.sum(jnp.where(same & (along < down), 1.0, 0.0), axis=1, keepdims=True)
    rank_row = jnp.sum(jnp.where(same & (down < along), 1.0, 0.0), axis=0, keepdims=True)
    span = 2 * height * count
    column = iota((1, span), 1)
    owner = lax.rem(column, height * count) // height
    code = jnp.sum(
        jnp.where(iota((count, span), 0) == owner, goal * 16.0 + rank * 4.0, 0.0),
        axis=0, keepdims=True,
    ).astype(jnp.int32)
    code = code + column // (height * count) * 8 + lax.rem(column, height)
    source = jnp.concatenate([blocks_ref[:, :256], blocks_ref[:, 256:]], axis=0)

    def chunk(step, carry):
        pick = (iota((512, span), 0) + step * 512 == code).astype(F32).astype(BF16)
        rows = jnp.dot(pick, source, preferred_element_type=F32).astype(BF16)
        out_ref[pl.ds(step * 32, 32)] = rows.reshape(32, 16, 256)
        return carry

    lax.fori_loop(0, total // 32, chunk, 0)
    slot_row = goal_row * 2.0 + rank_row
    offset_row = offset_ref[...].astype(F32)
    wanted = (2 * iota((total, count), 0)).astype(F32)
    first, second = [
        jnp.sum(jnp.where(wanted + r == slot_row, offset_row, 0.0), axis=1, keepdims=True)
        for r in (0.0, 1.0)
    ]
    lane = iota((total, 128), 1)
    spots = jnp.where(lane % 8 < 4, first, second) + (lane % 4).astype(F32)
    spot_ref[:, 0, :] = spots


def place_blocks(total, in_ref, spot_ref, frame_rows):
    span = total * 16
    spots = jnp.concatenate([spot_ref[:, 0, :]] * (span // 128), axis=1)
    column = iota((total, span), 1)
    spot = jnp.sum(jnp.where(column // 16 == iota((total, span), 0), spots, 0.0), axis=0, keepdims=True)
    spot = spot.astype(jnp.int32)
    lands = iota((frame_rows, span), 0) == spot
    upper = iota((1, span), 1) // 8 % 2
    rows = in_ref[...].reshape(span, 256)
    halves = [
        jnp.dot((lands & (upper == h)).astype(F32).astype(BF16), rows, preferred_element_type=F32)
        for h in range(2)
    ]
    return jnp.concatenate(halves, axis=1).astype(BF16)


def whole_kernel(
    total, corner_ref, count_ref, blocks_ref, route_ref, offset_ref, warp_ref, science_ref,
    cols_ref, rows_ref, prior_ref,
    difference_ref, residual_ref, solution_ref,
    out_ref, in_ref, spot_out_ref, spot_in_ref, edge_ref, ext_ref, pick_rows_ref, pick_columns_ref,
    sc_ref, sr_ref, x2_ref, field_ref, poly_ref, target_ref, gram_ref,
    tile_ref, part_ref, own_ref, sum_ref,
    fc_ref, fr_ref, across_ref, conv_ref, system_ref, answer_ref, piece_ref,
    block_sems, spot_sems, up_sems, down_sems, part_sems, sum_sems,
):
    me = lax.axis_index("ccd") * lax.axis_size("strip") + lax.axis_index("strip")
    height = science_ref.shape[0]
    barrier = pltpu.get_barrier_semaphore()

    def greet(step, carry):
        peer = lax.rem(me + step, total)
        pl.semaphore_signal(barrier, inc=1, device_id=coords(peer), device_id_type=MESH)
        return carry

    lax.fori_loop(1, total, greet, 0)
    pack(total, blocks_ref, route_ref, offset_ref, out_ref, spot_out_ref)
    in_ref[me] = out_ref[me]
    spot_in_ref[me] = spot_out_ref[me]
    pl.semaphore_wait(barrier, total - 1)

    def deliver(step, carry):
        peer = lax.rem(me + step, total)
        send(spot_out_ref.at[peer], spot_in_ref.at[me], spot_sems.at[0], spot_sems.at[1], peer)
        send(out_ref.at[peer], in_ref.at[me], block_sems.at[0], block_sems.at[1], peer)
        return carry

    lax.fori_loop(1, total, deliver, 0)
    first_row, total_rows = me * height, total * height
    prepare_stamps(
        first_row, total_rows, corner_ref, count_ref, science_ref,
        pick_rows_ref, pick_columns_ref, field_ref, poly_ref, target_ref,
    )
    build_stamp_bands(cols_ref, rows_ref, sc_ref, sr_ref)
    build_full_bands(cols_ref, rows_ref, fc_ref, fr_ref)
    most = pl.ds(0, total - 1)
    await_bytes(spot_in_ref.at[most], spot_sems.at[1])
    await_bytes(in_ref.at[most], block_sems.at[1])
    frame = place_blocks(total, in_ref, spot_in_ref, warp_ref.shape[1])
    template = jnp.dot(warp_ref[...], frame, preferred_element_type=F32).astype(BF16).astype(F32)
    template = jnp.concatenate([template, jnp.zeros((height, 2 * LP), F32)], axis=1)
    template = pltpu.roll(template, LP, 1)
    ext_ref[RP : RP + height, :] = template.astype(BF16)

    @pl.when(me < total - 1)
    def _():
        send(ext_ref.at[pl.ds(height, RP)], edge_ref.at[0], up_sems.at[0], up_sems.at[1], me + 1)

    @pl.when(me > 0)
    def _():
        send(ext_ref.at[pl.ds(RP, RP)], edge_ref.at[1], down_sems.at[0], down_sems.at[1], me - 1)

    await_bytes(spot_out_ref.at[most], spot_sems.at[0])
    await_bytes(out_ref.at[most], block_sems.at[0])
    blank = jnp.zeros((RP, ext_ref.shape[1]), F32)
    ext_ref[:RP, :] = blank.astype(BF16)
    ext_ref[RP + height :, :] = blank.astype(BF16)

    @pl.when(me > 0)
    def _():
        await_bytes(edge_ref.at[0], up_sems.at[1])
        ext_ref[:RP, :] = edge_ref[0]
        await_bytes(edge_ref.at[1], down_sems.at[0])

    @pl.when(me < total - 1)
    def _():
        await_bytes(edge_ref.at[1], down_sems.at[1])
        ext_ref[RP + height :, :] = edge_ref[1]
        await_bytes(edge_ref.at[0], up_sems.at[0])

    stamp_gram(
        ext_ref, pick_rows_ref, pick_columns_ref, sc_ref, sr_ref,
        x2_ref, field_ref, poly_ref, target_ref, gram_ref,
    )
    for t in range(NG // 8):
        tile_ref[t] = gram_ref[8 * t : 8 * t + 8, :128]
    for t in range(NG // 8, TILES):
        at = 128 + 8 * (t - NG // 8)
        tile_ref[t] = gram_ref[at : at + 8, 128:]

    def give(step, carry):
        t = lax.rem(me + step, TILES)

        @pl.when(t != me)
        def _():
            send(tile_ref.at[t], part_ref.at[me], part_sems.at[0], part_sems.at[1], t)

        return carry

    lax.fori_loop(0, TILES, give, 0)
    full_convolution(ext_ref, fc_ref, fr_ref, across_ref, conv_ref, 0, NK // 2)

    @pl.when(me < TILES)
    def _():
        part_ref[me] = tile_ref[me]
        await_bytes(part_ref.at[most], part_sems.at[1])
        own_ref[...] = jnp.sum(part_ref[...], axis=0)
        sum_ref[me] = own_ref[...]

        def spread(step, carry):
            peer = lax.rem(me + step, total)
            send(own_ref, sum_ref.at[me], sum_sems.at[0], sum_sems.at[1], peer)
            return carry

        lax.fori_loop(1, total, spread, 0)

    full_convolution(ext_ref, fc_ref, fr_ref, across_ref, conv_ref, NK // 2, NK)

    @pl.when(me < TILES)
    def _():
        await_bytes(sum_ref.at[pl.ds(0, TILES - 1)], sum_sems.at[1])
        await_bytes(tile_ref.at[pl.ds(0, TILES - 1)], part_sems.at[0])
        await_bytes(part_ref.at[most], sum_sems.at[0])

    @pl.when(me >= TILES)
    def _():
        await_bytes(sum_ref, sum_sems.at[1])
        await_bytes(tile_ref, part_sems.at[0])

    solve(sum_ref, prior_ref, system_ref, answer_ref, solution_ref)
    stamp_residuals(answer_ref, field_ref, poly_ref, target_ref, piece_ref, residual_ref)
    subtract(first_row, total_rows, science_ref, conv_ref, answer_ref, difference_ref)


VM = pl.BlockSpec(memory_space=pltpu.VMEM)
SM = pl.BlockSpec(memory_space=pltpu.SMEM)


STAMP_SCRATCH = [
    pltpu.VMEM((NK, 128, 256), BF16),
    pltpu.VMEM((NK, 64, 128), BF16),
    pltpu.VMEM((128, 256), BF16),
    pltpu.VMEM((KP, 64, 128), F32),
    pltpu.VMEM((8, 64, 128), F32),
    pltpu.VMEM((16, 64, 128), F32),
]


def padded_taps(taps):
    return jnp.pad(taps.astype(F32), ((0, KP - taps.shape[0]), (0, 256 - taps.shape[1])))


def local(
    coadd_blocks, block_route, block_offset, warp_matrix, science, basis_columns, basis_rows,
    stamp_corner, stamp_count, kernel_prior,
):
    total = lax.axis_size("ccd") * lax.axis_size("strip")
    height, width = science.shape
    rows, columns = height + 2 * RP, width + 2 * LP
    pair = pltpu.SemaphoreType.DMA((2,))
    prior = jnp.pad(kernel_prior[None, :], ((0, 0), (0, 256 - kernel_prior.shape[0])))
    difference, residual, answer = pl.pallas_call(
        functools.partial(whole_kernel, total),
        out_shape=(
            jax.ShapeDtypeStruct((height, width), F32),
            jax.ShapeDtypeStruct((8, 8, 128), F32),
            jax.ShapeDtypeStruct((1, 256), F32),
        ),
        in_specs=[SM, SM] + [VM] * 8,
        out_specs=(VM, VM, VM),
        scratch_shapes=[
            pltpu.VMEM((total, 16, 256), BF16),
            pltpu.VMEM((total, 16, 256), BF16),
            pltpu.VMEM((total, 1, 128), F32),
            pltpu.VMEM((total, 1, 128), F32),
            pltpu.VMEM((2, RP, columns), BF16),
            pltpu.VMEM((rows, columns), BF16),
            pltpu.VMEM((512, rows), BF16),
            pltpu.VMEM((8, columns, 128), BF16),
        ]
        + STAMP_SCRATCH
        + [
            pltpu.VMEM((NG, 256), F32),
            pltpu.VMEM((TILES, 8, 128), F32),
            pltpu.VMEM((total, 8, 128), F32),
            pltpu.VMEM((8, 128), F32),
            pltpu.VMEM((TILES, 8, 128), F32),
            pltpu.VMEM((NK, 128, 256), BF16),
            pltpu.VMEM((NK, 128, 256), BF16),
            pltpu.VMEM((rows, width), BF16),
            pltpu.VMEM((NK, height, width), BF16),
            pltpu.VMEM((NF, 256), F32),
            pltpu.VMEM((NF, 128), F32),
            pltpu.VMEM((32, 128), F32),
        ]
        + [pair] * 6,
        compiler_params=pltpu.CompilerParams(
            vmem_limit_bytes=52 << 20, collective_id=0, has_side_effects=True
        ),
    )(
        stamp_corner, stamp_count, coadd_blocks, block_route, block_offset[None, :], warp_matrix,
        science, padded_taps(basis_columns), padded_taps(basis_rows), prior,
    )
    return (
        difference,
        residual.reshape(8, SS * SS),
        answer[0, : kernel_prior.shape[0]],
    )


def solution(mesh):
    split = P(("ccd", "strip"), None)
    flat = P(("ccd", "strip"))
    in_specs = (split, split, flat, split, split, P(), P(), split, flat, P())
    out_specs = (split, split, P())
    return jax.shard_map(local, mesh=mesh, in_specs=in_specs, out_specs=out_specs, check_vma=False)
```

```python
import functools

import jax
import jax.numpy as jnp
from jax import lax
from jax.experimental import pallas as pl
from jax.experimental.pallas import tpu as pltpu
from jax.sharding import PartitionSpec as P

SS = 32
NK = 21
KP = 24
NF = 6 * KP
PIVOTS = 4
NG = NF + 16
LP = 64
RP = 16
NT = (((1,), (1,)), ((), ()))
F32 = jnp.float32
BF16 = jnp.bfloat16


def iota(shape, dim):
    return lax.broadcasted_iota(jnp.int32, shape, dim)


def toeplitz(taps_ref, k):
    row = taps_ref[pl.ds(k, 1), :]
    return pltpu.roll(jnp.broadcast_to(row, (16, 256)), 0, 1, stride=1, stride_axis=0)


def build_stamp_bands(cols_ref, rows_ref, sc_ref, sr_ref):
    def one(k, carry):
        col, row = toeplitz(cols_ref, k), toeplitz(rows_ref, k)
        for s in range(4):
            for g in range(2):
                shift = 64 * s + 16 * g
                value = col if shift == 0 else pltpu.roll(col, shift, 1)
                sc_ref[k, 32 * s + 16 * g : 32 * s + 16 * g + 16, :] = value.astype(BF16)
        for h in range(2):
            for g in range(2):
                value = pltpu.roll(row, 64 * h + 16 * g + 6, 1)[:, :128]
                sr_ref[k, 32 * h + 16 * g : 32 * h + 16 * g + 16, :] = value.astype(BF16)
        return carry

    lax.fori_loop(0, NK, one, 0)


def build_full_bands(cols_ref, rows_ref, fc_ref, fr_ref):
    def one(k, carry):
        col, row = toeplitz(cols_ref, k), toeplitz(rows_ref, k)
        for g in range(8):
            fc_ref[k, 16 * g : 16 * g + 16, :] = pltpu.roll(col, LP - 10 + 16 * g, 1).astype(BF16)
            fr_ref[k, 16 * g : 16 * g + 16, :] = pltpu.roll(row, 6 + 16 * g, 1).astype(BF16)
        return carry

    lax.fori_loop(0, NK, one, 0)


def prepare_stamps(
    first_row, total_rows, corner_ref, count_ref, science_ref,
    pick_rows_ref, pick_columns_ref, field_ref, poly_ref, target_ref,
):
    height, width = science_ref.shape
    full = pick_columns_ref.shape[1]
    live = jnp.zeros((64, 128), F32)
    rows = jnp.zeros((64, 128), jnp.int32)
    columns = jnp.zeros((64, 128), jnp.int32)
    group = iota((1, 128), 1) // 32
    half_of = iota((64, 128), 0) // 32
    lag = iota((64, height + 2 * RP), 1) - iota((64, height + 2 * RP), 0)
    short = iota((32, height), 1) - iota((32, height), 0)
    left = iota((full, 128), 0) - iota((full, 128), 1) % 64 - (LP - 10)
    side = iota((full, 128), 1) // 64
    near = iota((width, 128), 0) - iota((width, 128), 1) % 32
    value = science_ref[...]
    parts = []
    for part in range(3):
        parts.append(value.astype(BF16))
        value = value - parts[-1].astype(F32)
    picks = []
    for slot in range(8):
        a = corner_ref[slot, 0]
        e = corner_ref[slot, 1]
        picks.append((short == a).astype(F32))
        pick_rows_ref[64 * slot : 64 * slot + 64, :] = (lag == a).astype(F32).astype(BF16)
        pick_columns_ref[slot] = ((left == e) & (side == slot % 2)).astype(F32).astype(BF16)
        here = (half_of == slot // 4) & (group == slot % 4)
        live = jnp.where(here, (slot < count_ref[0]).astype(F32), live)
        rows = jnp.where(here, a, rows)
        columns = jnp.where(here, e, columns)
    picks = jnp.concatenate(picks, axis=0).astype(BF16)
    picked = jnp.dot(picks, jnp.concatenate(parts, axis=1), preferred_element_type=F32).astype(BF16)
    for h in range(2):
        total = jnp.zeros((96, 128), F32)
        for s in range(4):
            slot = h * 4 + s
            stack = jnp.concatenate(
                [
                    picked[32 * slot : 32 * slot + 32, width * part : width * part + width]
                    for part in range(3)
                ],
                axis=0,
            )
            chosen = ((near == corner_ref[slot, 1]) & (group == s)).astype(F32).astype(BF16)
            total = total + jnp.dot(stack, chosen, preferred_element_type=F32)
        for part in range(3):
            at = slice(32 * h, 32 * h + 32)
            target_ref[part, at, :] = total[32 * part : 32 * part + 32] * live[at]
    for part in range(3, 16):
        target_ref[part] = jnp.zeros((64, 128), F32)
    rows = rows + iota((64, 128), 0) % 32 + first_row
    columns = columns + iota((64, 128), 1) % 32
    y = (2 * rows + 1).astype(F32) / total_rows - 1.0
    x = (2 * columns + 1).astype(F32) / width - 1.0
    poly_ref[0] = jnp.ones_like(x)
    poly_ref[1] = x
    poly_ref[2] = y
    poly_ref[3] = 1.5 * x * x - 0.5
    poly_ref[4] = x * y
    poly_ref[5] = 1.5 * y * y - 0.5
    field_ref[NK] = live
    for k in range(NK + 1, KP):
        field_ref[k] = jnp.zeros((64, 128), F32)


def stamp_gram(
    ext_ref, pick_rows_ref, pick_columns_ref, sc_ref, sr_ref,
    x2_ref, field_ref, poly_ref, target_ref, gram_ref,
):
    picked = jnp.dot(pick_rows_ref[...], ext_ref[...], preferred_element_type=F32).astype(BF16)
    for pair in range(4):
        window = sum(
            jnp.dot(
                picked[64 * slot : 64 * slot + 64], pick_columns_ref[slot],
                preferred_element_type=F32,
            )
            for slot in (2 * pair, 2 * pair + 1)
        )
        at = 128 * (pair % 2)
        x2_ref[64 * (pair // 2) : 64 * (pair // 2) + 64, at : at + 128] = window.astype(BF16)
    live = field_ref[NK]

    def convolve(k, carry):
        across = lax.dot_general(x2_ref[...], sc_ref[k], NT, preferred_element_type=F32)
        down = jnp.dot(sr_ref[k], across.astype(BF16), preferred_element_type=F32)
        field_ref[k] = down.astype(BF16).astype(F32) * live
        return carry

    lax.fori_loop(0, NK, convolve, 0)
    gram_ref[...] = jnp.zeros_like(gram_ref)

    def row_features(q):
        field = field_ref[:, q, :]
        parts = [field]
        for p in range(1, 6):
            parts.append(field * poly_ref[p, pl.ds(q, 1), :])
        parts.append(target_ref[:, q, :])
        return jnp.concatenate(parts, axis=0).astype(BF16)

    def add(step, carry):
        both = jnp.concatenate([row_features(2 * step), row_features(2 * step + 1)], axis=1)
        gram_ref[:, :NG] += lax.dot_general(both, both, NT, preferred_element_type=F32)
        return carry

    lax.fori_loop(0, 32, add, 0)


def full_convolution(ext_ref, fc_ref, fr_ref, across_ref, conv_ref, first, last):
    tiles = conv_ref.shape[2] // 128
    halves = conv_ref.shape[1] // 128

    def one(k, carry):
        for t in range(tiles):
            across_ref[:, 128 * t : 128 * t + 128] = lax.dot_general(
                ext_ref[:, 128 * t : 128 * t + 256], fc_ref[k], NT, preferred_element_type=F32
            ).astype(BF16)
        for t in range(halves):
            conv_ref[k, 128 * t : 128 * t + 128, :] = jnp.dot(
                fr_ref[k, :, :160],
                across_ref[128 * t : 128 * t + 160, :],
                preferred_element_type=F32,
            ).astype(BF16)
        return carry

    lax.fori_loop(first, last, one, 0)


def solve(sum_ref, prior_ref, system_ref, answer_ref, solution_ref):
    at = iota((NF, 256), 0)
    lane = iota((NF, 256), 1)
    left = sum_ref[: NG // 8].reshape(NG, 128)
    corner = sum_ref[NG // 8 :].reshape(NG - 128, 128)
    edge = jnp.concatenate([left[128:], jnp.zeros((256 - NG, 128), F32)], axis=0)
    right = jnp.concatenate([edge.T, corner[: NF - 128]], axis=0)
    wide = jnp.concatenate([left[:NF], right], axis=1)
    pixels = left[NK : NK + 1, NK : NK + 1]
    order = (at % KP) * 6 + at // KP
    used = at % KP <= NK
    right = jnp.sum(jnp.where((lane >= NF) & (lane < NF + 3), wide, 0.0), axis=1, keepdims=True)
    prior = jnp.sum(
        jnp.where((lane == order) & used, prior_ref[...], 0.0), axis=1, keepdims=True
    )
    right = right / pixels + prior
    body = jnp.where(used & (lane % KP <= NK) & (lane < NF), wide / pixels, 0.0)
    body = body + (at == lane).astype(F32)
    system_ref[...] = jnp.where((lane == NF) & used, right, body)

    def eliminate(step, carry):
        first = pl.multiple_of(step * PIVOTS, PIVOTS)
        matrix = system_ref[...]
        each = range(PIVOTS)
        rows = [system_ref[pl.ds(first + i, 1), :] for i in each]
        pick = lambda v, i: jnp.sum(
            jnp.where(lane[: v.shape[0]] == first + i, v, 0.0), axis=1, keepdims=True
        )
        columns = [pick(matrix, i) for i in each]
        heads = [[pick(rows[i], m) for m in each] for i in each]
        for i in each:
            factor = jnp.where(at[:, :1] == first + i, 0.0, columns[i] / heads[i][i])
            matrix = matrix - factor * rows[i]
            for m in range(i + 1, PIVOTS):
                columns[m] = columns[m] - factor * heads[i][m]
                scale = heads[m][i] / heads[i][i]
                rows[m] = rows[m] - scale * rows[i]
                heads[m] = [heads[m][n] - scale * heads[i][n] for n in each]
        system_ref[...] = matrix
        return carry

    lax.fori_loop(0, NF // PIVOTS, eliminate, 0)
    matrix = system_ref[...]
    top = jnp.sum(jnp.where(lane == NF, matrix, 0.0), axis=1, keepdims=True)
    diagonal = jnp.sum(jnp.where(lane == at, matrix, 0.0), axis=1, keepdims=True)
    answer = top / diagonal
    answer_ref[...] = jnp.broadcast_to(answer, (NF, 128))
    solution_ref[...] = jnp.sum(
        jnp.where((lane == order) & used, answer, 0.0), axis=0, keepdims=True
    )


def subtract(
    first_row, total_rows, science_ref, conv_ref, answer_ref, difference_ref,
):
    height, width = science_ref.shape
    x = (2 * iota((1, width), 1) + 1).astype(F32) / width - 1.0
    x2 = 1.5 * x * x - 0.5

    def band(step, carry):
        start = pl.multiple_of(step * 16, 16)
        y = (2 * (first_row + start + iota((16, 128), 0)) + 1).astype(F32) / total_rows - 1.0
        y2 = 1.5 * y * y - 0.5

        def term(k):
            c = [answer_ref[p * KP + k : p * KP + k + 1, :] for p in range(6)]
            flat, slope, curve = c[0] + c[2] * y + c[5] * y2, c[1] + c[4] * y, c[3]
            spread = lambda v: jnp.concatenate([v] * (width // 128), axis=1)
            return spread(flat), spread(slope), spread(curve)

        flat, slope, curve = term(NK)
        curve = jnp.broadcast_to(curve, flat.shape)
        for k in range(NK):
            value = conv_ref[k, pl.ds(start, 16), :].astype(F32)
            f, s, c = term(k)
            flat, slope, curve = flat + value * f, slope + value * s, curve + value * c
        matched = flat + slope * x + curve * x2
        difference_ref[pl.ds(start, 16), :] = science_ref[pl.ds(start, 16), :] - matched
        return carry

    lax.fori_loop(0, height // 16, band, 0)


def stamp_residuals(answer_ref, field_ref, poly_ref, target_ref, piece_ref, residual_ref):
    value = target_ref[0] + target_ref[1] + target_ref[2]
    for k in range(NK + 1):
        weight = answer_ref[k : k + 1, :]
        for p in range(1, 6):
            weight = weight + answer_ref[p * KP + k : p * KP + k + 1, :] * poly_ref[p]
        value = value - field_ref[k] * weight
    group = iota((8, 128), 1) // 32
    for slot in range(8):
        s = slot % 4
        piece = value[32 * (slot // 4) : 32 * (slot // 4) + 32]
        piece_ref[...] = pltpu.roll(piece, 128 - 32 * s, 1) if s else piece
        result = jnp.zeros((8, 128), F32)
        for m in range(4):
            part = piece_ref[pl.ds(m, 8, stride=4), :]
            part = pltpu.roll(part, 32 * m, 1) if m else part
            result = jnp.where(group == m, part, result)
        residual_ref[slot] = result


MESH = pl.DeviceIdType.MESH
TILES = NG // 8 + (NG - 128) // 8


def coords(device):
    return (device // lax.axis_size("strip"), lax.rem(device, lax.axis_size("strip")))


def send(src, dst, send_sem, recv_sem, device):
    pltpu.make_async_remote_copy(
        src_ref=src, dst_ref=dst, send_sem=send_sem, recv_sem=recv_sem,
        device_id=coords(device), device_id_type=MESH,
    ).start()


def await_bytes(ref, sem):
    pltpu.make_async_copy(ref, ref, sem).wait()


def pack(total, blocks_ref, route_ref, offset_ref, out_ref, spot_ref):
    count = route_ref.shape[0]
    height = blocks_ref.shape[0] // count
    goal = route_ref[...].astype(F32)
    down, along = iota((count, count), 0), iota((count, count), 1)
    goal_row = jnp.sum(jnp.where(down == along, goal, 0.0), axis=0, keepdims=True)
    same = goal == goal_row
    rank = jnp.sum(jnp.where(same & (along < down), 1.0, 0.0), axis=1, keepdims=True)
    rank_row = jnp.sum(jnp.where(same & (down < along), 1.0, 0.0), axis=0, keepdims=True)
    span = 2 * height * count
    column = iota((1, span), 1)
    owner = lax.rem(column, height * count) // height
    code = jnp.sum(
        jnp.where(iota((count, span), 0) == owner, goal * 16.0 + rank * 4.0, 0.0),
        axis=0, keepdims=True,
    ).astype(jnp.int32)
    code = code + column // (height * count) * 8 + lax.rem(column, height)
    source = jnp.concatenate([blocks_ref[:, :256], blocks_ref[:, 256:]], axis=0)

    def chunk(step, carry):
        pick = (iota((512, span), 0) + step * 512 == code).astype(F32).astype(BF16)
        rows = jnp.dot(pick, source, preferred_element_type=F32).astype(BF16)
        out_ref[pl.ds(step * 32, 32)] = rows.reshape(32, 16, 256)
        return carry

    lax.fori_loop(0, total // 32, chunk, 0)
    slot_row = goal_row * 2.0 + rank_row
    offset_row = offset_ref[...].astype(F32)
    wanted = (2 * iota((total, count), 0)).astype(F32)
    first, second = [
        jnp.sum(jnp.where(wanted + r == slot_row, offset_row, 0.0), axis=1, keepdims=True)
        for r in (0.0, 1.0)
    ]
    lane = iota((total, 128), 1)
    spots = jnp.where(lane % 8 < 4, first, second) + (lane % 4).astype(F32)
    spot_ref[:, 0, :] = spots


def place_blocks(total, in_ref, spot_ref, frame_rows):
    span = total * 16
    spots = jnp.concatenate([spot_ref[:, 0, :]] * (span // 128), axis=1)
    column = iota((total, span), 1)
    spot = jnp.sum(jnp.where(column // 16 == iota((total, span), 0), spots, 0.0), axis=0, keepdims=True)
    spot = spot.astype(jnp.int32)
    lands = iota((frame_rows, span), 0) == spot
    upper = iota((1, span), 1) // 8 % 2
    rows = in_ref[...].reshape(span, 256)
    halves = [
        jnp.dot((lands & (upper == h)).astype(F32).astype(BF16), rows, preferred_element_type=F32)
        for h in range(2)
    ]
    return jnp.concatenate(halves, axis=1).astype(BF16)


def whole_kernel(
    total, corner_ref, count_ref, blocks_ref, route_ref, offset_ref, warp_ref, science_ref,
    cols_ref, rows_ref, prior_ref,
    difference_ref, residual_ref, solution_ref,
    out_ref, in_ref, spot_out_ref, spot_in_ref, edge_ref, ext_ref, pick_rows_ref, pick_columns_ref,
    sc_ref, sr_ref, x2_ref, field_ref, poly_ref, target_ref, gram_ref,
    tile_ref, part_ref, own_ref, sum_ref,
    fc_ref, fr_ref, across_ref, conv_ref, system_ref, answer_ref, piece_ref,
    block_sems, spot_sems, up_sems, down_sems, part_sems, sum_sems,
):
    me = lax.axis_index("ccd") * lax.axis_size("strip") + lax.axis_index("strip")
    height = science_ref.shape[0]
    barrier = pltpu.get_barrier_semaphore()

    def greet(step, carry):
        peer = lax.rem(me + step, total)
        pl.semaphore_signal(barrier, inc=1, device_id=coords(peer), device_id_type=MESH)
        return carry

    lax.fori_loop(1, total, greet, 0)
    pack(total, blocks_ref, route_ref, offset_ref, out_ref, spot_out_ref)
    in_ref[me] = out_ref[me]
    spot_in_ref[me] = spot_out_ref[me]
    pl.semaphore_wait(barrier, total - 1)

    def deliver(step, carry):
        peer = lax.rem(me + step, total)
        send(spot_out_ref.at[peer], spot_in_ref.at[me], spot_sems.at[0], spot_sems.at[1], peer)
        send(out_ref.at[peer], in_ref.at[me], block_sems.at[0], block_sems.at[1], peer)
        return carry

    lax.fori_loop(1, total, deliver, 0)
    first_row, total_rows = me * height, total * height
    prepare_stamps(
        first_row, total_rows, corner_ref, count_ref, science_ref,
        pick_rows_ref, pick_columns_ref, field_ref, poly_ref, target_ref,
    )
    build_stamp_bands(cols_ref, rows_ref, sc_ref, sr_ref)
    build_full_bands(cols_ref, rows_ref, fc_ref, fr_ref)
    most = pl.ds(0, total - 1)
    await_bytes(spot_in_ref.at[most], spot_sems.at[1])
    await_bytes(in_ref.at[most], block_sems.at[1])
    frame = place_blocks(total, in_ref, spot_in_ref, warp_ref.shape[1])
    template = jnp.dot(warp_ref[...], frame, preferred_element_type=F32).astype(BF16).astype(F32)
    template = jnp.concatenate([template, jnp.zeros((height, 2 * LP), F32)], axis=1)
    template = pltpu.roll(template, LP, 1)
    ext_ref[RP : RP + height, :] = template.astype(BF16)

    @pl.when(me < total - 1)
    def _():
        send(ext_ref.at[pl.ds(height, RP)], edge_ref.at[0], up_sems.at[0], up_sems.at[1], me + 1)

    @pl.when(me > 0)
    def _():
        send(ext_ref.at[pl.ds(RP, RP)], edge_ref.at[1], down_sems.at[0], down_sems.at[1], me - 1)

    await_bytes(spot_out_ref.at[most], spot_sems.at[0])
    await_bytes(out_ref.at[most], block_sems.at[0])
    blank = jnp.zeros((RP, ext_ref.shape[1]), F32)
    ext_ref[:RP, :] = blank.astype(BF16)
    ext_ref[RP + height :, :] = blank.astype(BF16)

    @pl.when(me > 0)
    def _():
        await_bytes(edge_ref.at[0], up_sems.at[1])
        ext_ref[:RP, :] = edge_ref[0]
        await_bytes(edge_ref.at[1], down_sems.at[0])

    @pl.when(me < total - 1)
    def _():
        await_bytes(edge_ref.at[1], down_sems.at[1])
        ext_ref[RP + height :, :] = edge_ref[1]
        await_bytes(edge_ref.at[0], up_sems.at[0])

    stamp_gram(
        ext_ref, pick_rows_ref, pick_columns_ref, sc_ref, sr_ref,
        x2_ref, field_ref, poly_ref, target_ref, gram_ref,
    )
    for t in range(NG // 8):
        tile_ref[t] = gram_ref[8 * t : 8 * t + 8, :128]
    for t in range(NG // 8, TILES):
        at = 128 + 8 * (t - NG // 8)
        tile_ref[t] = gram_ref[at : at + 8, 128:]

    def give(step, carry):
        t = lax.rem(me + step, TILES)

        @pl.when(t != me)
        def _():
            send(tile_ref.at[t], part_ref.at[me], part_sems.at[0], part_sems.at[1], t)

        return carry

    lax.fori_loop(0, TILES, give, 0)
    full_convolution(ext_ref, fc_ref, fr_ref, across_ref, conv_ref, 0, NK // 2)

    @pl.when(me < TILES)
    def _():
        part_ref[me] = tile_ref[me]
        await_bytes(part_ref.at[most], part_sems.at[1])
        own_ref[...] = jnp.sum(part_ref[...], axis=0)
        sum_ref[me] = own_ref[...]

        def spread(step, carry):
            peer = lax.rem(me + step, total)
            send(own_ref, sum_ref.at[me], sum_sems.at[0], sum_sems.at[1], peer)
            return carry

        lax.fori_loop(1, total, spread, 0)

    full_convolution(ext_ref, fc_ref, fr_ref, across_ref, conv_ref, NK // 2, NK)

    @pl.when(me < TILES)
    def _():
        await_bytes(sum_ref.at[pl.ds(0, TILES - 1)], sum_sems.at[1])
        await_bytes(tile_ref.at[pl.ds(0, TILES - 1)], part_sems.at[0])
        await_bytes(part_ref.at[most], sum_sems.at[0])

    @pl.when(me >= TILES)
    def _():
        await_bytes(sum_ref, sum_sems.at[1])
        await_bytes(tile_ref, part_sems.at[0])

    solve(sum_ref, prior_ref, system_ref, answer_ref, solution_ref)
    stamp_residuals(answer_ref, field_ref, poly_ref, target_ref, piece_ref, residual_ref)
    subtract(first_row, total_rows, science_ref, conv_ref, answer_ref, difference_ref)


VM = pl.BlockSpec(memory_space=pltpu.VMEM)
SM = pl.BlockSpec(memory_space=pltpu.SMEM)


STAMP_SCRATCH = [
    pltpu.VMEM((NK, 128, 256), BF16),
    pltpu.VMEM((NK, 64, 128), BF16),
    pltpu.VMEM((128, 256), BF16),
    pltpu.VMEM((KP, 64, 128), F32),
    pltpu.VMEM((8, 64, 128), F32),
    pltpu.VMEM((16, 64, 128), F32),
]


def padded_taps(taps):
    return jnp.pad(taps.astype(F32), ((0, KP - taps.shape[0]), (0, 256 - taps.shape[1])))


def local(
    coadd_blocks, block_route, block_offset, warp_matrix, science, basis_columns, basis_rows,
    stamp_corner, stamp_count, kernel_prior,
):
    total = lax.axis_size("ccd") * lax.axis_size("strip")
    height, width = science.shape
    rows, columns = height + 2 * RP, width + 2 * LP
    pair = pltpu.SemaphoreType.DMA((2,))
    prior = jnp.pad(kernel_prior[None, :], ((0, 0), (0, 256 - kernel_prior.shape[0])))
    difference, residual, answer = pl.pallas_call(
        functools.partial(whole_kernel, total),
        out_shape=(
            jax.ShapeDtypeStruct((height, width), F32),
            jax.ShapeDtypeStruct((8, 8, 128), F32),
            jax.ShapeDtypeStruct((1, 256), F32),
        ),
        in_specs=[SM, SM] + [VM] * 8,
        out_specs=(VM, VM, VM),
        scratch_shapes=[
            pltpu.VMEM((total, 16, 256), BF16),
            pltpu.VMEM((total, 16, 256), BF16),
            pltpu.VMEM((total, 1, 128), F32),
            pltpu.VMEM((total, 1, 128), F32),
            pltpu.VMEM((2, RP, columns), BF16),
            pltpu.VMEM((rows, columns), BF16),
            pltpu.VMEM((512, rows), BF16),
            pltpu.VMEM((8, columns, 128), BF16),
        ]
        + STAMP_SCRATCH
        + [
            pltpu.VMEM((NG, 256), F32),
            pltpu.VMEM((TILES, 8, 128), F32),
            pltpu.VMEM((total, 8, 128), F32),
            pltpu.VMEM((8, 128), F32),
            pltpu.VMEM((TILES, 8, 128), F32),
            pltpu.VMEM((NK, 128, 256), BF16),
            pltpu.VMEM((NK, 128, 256), BF16),
            pltpu.VMEM((rows, width), BF16),
            pltpu.VMEM((NK, height, width), BF16),
            pltpu.VMEM((NF, 256), F32),
            pltpu.VMEM((NF, 128), F32),
            pltpu.VMEM((32, 128), F32),
        ]
        + [pair] * 6,
        compiler_params=pltpu.CompilerParams(
            vmem_limit_bytes=52 << 20, collective_id=0, has_side_effects=True
        ),
    )(
        stamp_corner, stamp_count, coadd_blocks, block_route, block_offset[None, :], warp_matrix,
        science, padded_taps(basis_columns), padded_taps(basis_rows), prior,
    )
    return (
        difference,
        residual.reshape(8, SS * SS),
        answer[0, : kernel_prior.shape[0]],
    )


def solution(mesh):
    split = P(("ccd", "strip"), None)
    flat = P(("ccd", "strip"))
    in_specs = (split, split, flat, split, split, P(), P(), split, flat, P())
    out_specs = (split, split, P())
    return jax.shard_map(local, mesh=mesh, in_specs=in_specs, out_specs=out_specs, check_vma=False)
```
